32 devices in a mesh: seq: 8 (over z, y), tensor: 2 (over x), group: 2 (over core).
Axes of the slice: x: 2, y: 2, z: 4, core: 2. Of those that a mesh axis runs over, the one named last changes fastest.
Arguments:
- prefill_queries: bfloat16 [512, 8192], P(None, 'tensor'), may hold values from -6 to 6
- cached_keys: bfloat16 [16384, 1024], P(('seq', 'group'), 'tensor'), may hold values from -6 to 6
- cached_values: bfloat16 [16384, 1024], P(('seq', 'group'), 'tensor'), may hold values from -6 to 6
- span_keys: bfloat16 [512, 1024], P(('seq', 'group'), 'tensor'), may hold values from -6 to 6
- span_values: bfloat16 [512, 1024], P(('seq', 'group'), 'tensor'), may hold values from -6 to 6
- out_weight: bfloat16 [8192, 8192], P('tensor', 'seq'), may hold values from -0.0625 to 0.0625
- decode_queries: bfloat16 [4, 32, 8192], P(None, 'group', 'tensor'), may hold values from -6 to 6
- decode_keys: bfloat16 [32, 2048, 1024], P('group', 'seq', 'tensor'), may hold values from -6 to 6
- decode_values: bfloat16 [32, 2048, 1024], P('group', 'seq', 'tensor'), may hold values from -6 to 6
- new_keys: bfloat16 [4, 32, 1024], P(None, 'group', 'tensor'), may hold values from -6 to 6
- new_values: bfloat16 [4, 32, 1024], P(None, 'group', 'tensor'), may hold values from -6 to 6
- request_lengths: int32 [32], replicated, may hold values from 1 to 2048
- row_requests: int32 [32], P('group'), may hold values from 0 to 31
- block_table: int32 [128, 1], replicated, may hold values from 0 to 15; in each aligned block of 128 rows (0 to 127, 128 to 255, ...) at most 16 rows name the same one
Outputs:
- prefill_out: bfloat16 [512, 8192], P('group', ('seq', 'tensor'))
- decode_out: bfloat16 [4, 32, 8192], P(None, 'group', ('seq', 'tensor'))
- landed_keys: bfloat16 [16, 16, 4, 1024], P(('seq', 'group'), None, None, 'tensor')
- landed_values: bfloat16 [16, 16, 4, 1024], P(('seq', 'group'), None, None, 'tensor')
The draws below stay inside these ranges and needn't reach their ends.
Inputs may be any that keep to these rules, and one draw needn't show every extreme that they name: `block_table`: each owner receives at most 16 blocks, and some owner receives exactly 16; every owner receives at least one.
All inputs are finite; a program needn't handle non-finite values.
Results may differ from the reference program's by a relative error of at most 0.0052.
Values may be sent and summed in bfloat16 or wider, within the bound.
A program may use at most 128 MiB of HBM per device.

```python
import math
import jax
import jax.numpy as jnp
import numpy as np
from jax import lax

D = 8192
HEADS = 64
KV_HEADS = 8
HEAD = 128
SPAN = 512
BLOCK = 4
STEPS = 4
CONTEXT = 16384
OWNERS = 16
NBLOCKS = 128
MOST = 16
ROWS = 32
CTX_MAX = 2048
REQUESTS = 32


def base_field(key, shape):
    return jnp.clip(jax.random.normal(key, shape, jnp.float32), -6.0, 6.0)


def aligned_signs(key, salt, count):
    flips = jax.random.bernoulli(jax.random.fold_in(key, salt), 0.5, (count, HEAD))
    return jnp.where(flips, 1.0, -1.0).astype(jnp.float32)


def strength_table(order):
    levels = jnp.array([1.5, 2.0, 3.0, 4.0], jnp.float32)
    return levels[order % 4]


def prefill_plan():
    order = jnp.arange(8, dtype=jnp.int32)
    query_rows = order * (SPAN // 8) + 1
    heads = order * 9 % HEADS
    cached_rows = order * (CONTEXT // 8)
    return (order, query_rows, heads, cached_rows)


def decode_plan():
    count = ROWS // 4
    order = jnp.arange(count, dtype=jnp.int32)
    rows = order * 4
    heads = order * 9 % HEADS
    steps = order % STEPS
    return (order, rows, heads, steps)


def key_pair(signs, order):
    first = strength_table(order)[:, None] * signs
    second = first.at[:, 0].add(-4.0 * signs[:, 0])
    return (first, second)


def draw_prefill_queries(key, part):
    field = base_field(jax.random.fold_in(key, 11), (SPAN, HEADS * HEAD))
    order, query_rows, heads, cached_rows = prefill_plan()
    signs = aligned_signs(key, 4242, 8)
    columns = heads[:, None] * HEAD + jnp.arange(HEAD, dtype=jnp.int32)[None, :]
    field = field.at[query_rows[:, None], columns].set(6.0 * signs)
    return field.astype(jnp.bfloat16)


def draw_cached_keys(key, part):
    field = base_field(jax.random.fold_in(key, 12), (CONTEXT, KV_HEADS * HEAD))
    order, query_rows, heads, cached_rows = prefill_plan()
    signs = aligned_signs(key, 4242, 8)
    first, second = key_pair(signs, order)
    groups = heads // (HEADS // KV_HEADS)
    columns = groups[:, None] * HEAD + jnp.arange(HEAD, dtype=jnp.int32)[None, :]
    field = field.at[cached_rows[:, None], columns].set(first)
    field = field.at[(cached_rows + CONTEXT // 16)[:, None], columns].set(second)
    return field.astype(jnp.bfloat16)


def draw_decode_queries(key, part):
    field = base_field(jax.random.fold_in(key, 13), (STEPS, ROWS, HEADS * HEAD))
    order, rows, heads, steps = decode_plan()
    signs = aligned_signs(key, 4343, ROWS // 4)
    columns = heads[:, None] * HEAD + jnp.arange(HEAD, dtype=jnp.int32)[None, :]
    field = field.at[steps[:, None], rows[:, None], columns].set(6.0 * signs)
    return field.astype(jnp.bfloat16)


def draw_decode_keys(key, part):
    field = base_field(jax.random.fold_in(key, 14), (ROWS, CTX_MAX, KV_HEADS * HEAD))
    order, rows, heads, steps = decode_plan()
    signs = aligned_signs(key, 4343, ROWS // 4)
    first, second = key_pair(signs, order)
    groups = heads // (HEADS // KV_HEADS)
    columns = groups[:, None] * HEAD + jnp.arange(HEAD, dtype=jnp.int32)[None, :]
    field = field.at[rows[:, None], 0, columns].set(first)
    return field.astype(jnp.bfloat16)


def draw_new_keys(key, part):
    field = base_field(jax.random.fold_in(key, 15), (STEPS, ROWS, KV_HEADS * HEAD))
    order, rows, heads, steps = decode_plan()
    signs = aligned_signs(key, 4343, ROWS // 4)
    first, second = key_pair(signs, order)
    groups = heads // (HEADS // KV_HEADS)
    columns = groups[:, None] * HEAD + jnp.arange(HEAD, dtype=jnp.int32)[None, :]
    field = field.at[0, rows[:, None], columns].set(second)
    return field.astype(jnp.bfloat16)


def set_ends(drawn, stream_key, smallest, largest):
    shape = drawn.shape
    place = [jax.random.randint(jax.random.fold_in(stream_key, axis), (), 0, shape[axis]) for axis in range(len(shape))]
    drawn = drawn.at[tuple(place)].set(smallest)
    longest = shape.index(max(shape))
    place[longest] = (place[longest] + 1) % shape[longest]
    return drawn.at[tuple(place)].set(largest)


def shard_levels(key, dims, pieces, least, largest):
    level = 1.0
    for dim, shards_of in pieces:
        heights = jax.random.uniform(jax.random.fold_in(jax.random.fold_in(key, 6), dim), (shards_of,), jnp.float32, least / len(pieces), largest / len(pieces))
        level = level * jnp.repeat(jnp.exp(heights), dims[dim] // shards_of).reshape((-1,) + (1,) * (len(dims) - 1 - dim))
    return level


def deal_out(key, own, number, rows, count, top, reach, skew):
    ranking = jax.random.permutation(key, count)
    crowded, common = shares(count, rows * top, reach, skew, True), shares(count, rows * top, reach, skew, False)
    places = jnp.arange(count)

    def named(sizes, rotation):
        used = int((sizes > 0).sum())
        fixed = max(1, used // 4)
        moved = fixed + (places - fixed + rotation * (used - fixed)) % max(1, count - fixed)
        return jnp.zeros((count,), jnp.int32).at[ranking[jnp.where(places < fixed, places, moved)]].set(jnp.asarray(sizes, jnp.int32))

    sizes = jnp.where(number % 4 == 0, named(crowded, number // 4), named(common, number - number // 4 - 1))
    mixed = jax.random.permutation(jax.random.fold_in(own, 3), count)
    source_of, sink = mixed[0:count // 2 * 2:2], mixed[1:count // 2 * 2:2]
    slack = jnp.minimum(sizes[source_of] - 1, reach - sizes[sink]) // 2
    slack = jnp.where((source_of == ranking[0]) | (sink == ranking[0]) | (sizes[sink] == 0), 0, jnp.maximum(slack, 0))
    moved = jax.random.randint(jax.random.fold_in(own, 4), (count // 2,), 0, 1 << 20) % (slack + 1)
    sizes = sizes.at[source_of].add(-moved).at[sink].add(moved)
    labels = jnp.searchsorted(jnp.cumsum(sizes), jnp.arange(rows * top), side="right").astype(jnp.int32)
    grid = labels.reshape(top, rows).T
    grid = grid[jax.random.permutation(jax.random.fold_in(own, 1), rows)]
    rotation = jax.random.randint(jax.random.fold_in(own, 2), (rows, 1), 0, top)
    return jnp.take_along_axis(grid, (jnp.arange(top)[None, :] + rotation) % top, axis=1)


def shares(count, total, reach, slope, full):
    loads = [(1 << 20) // math.isqrt(rank ** slope) + 1 for rank in range(1, count + 1)]
    largest = reach if full else min(reach, max(-(-total // count), total * loads[0] // sum(loads)))
    least = 1 if total - largest >= count - 1 else 0
    counts, surplus = [largest] + [least] * (count - 1), total - largest - least * (count - 1)
    while surplus > 0:
        movable = [i for i in range(1, count) if counts[i] < largest] or [i for i in range(1, count) if counts[i] < reach]
        whole, left = sum([loads[i] for i in movable]), surplus
        for i in movable:
            extra = min(reach - counts[i], max(1, left * loads[i] // whole), surplus)
            counts[i] = counts[i] + extra
            surplus = surplus - extra
    return np.array(counts)


def noise(rng, extent, spread, reach, split=(), held_as=jnp.bfloat16):
    values = spread * jax.random.normal(rng, extent, jnp.float32)
    if split:
        values = values * shard_levels(rng, extent, split, -0.22, 0.18)
    return jnp.clip(values, -reach, reach).astype(held_as)


def setup_inputs(seed: int = 0) -> dict:
    splits = jax.random.split(jax.random.key(seed), 15)
    prefill_queries = draw_prefill_queries(jax.random.fold_in(splits[14], 71), 0)
    cached_keys = draw_cached_keys(jax.random.fold_in(splits[14], 71), 0)
    cached_values = noise(splits[2], (CONTEXT, KV_HEADS * HEAD), 1.0, 6.0, ((0, 16), (1, 2)))
    span_keys = noise(splits[3], (SPAN, KV_HEADS * HEAD), 1.0, 6.0, ((0, 16), (1, 2)))
    span_values = noise(splits[4], (SPAN, KV_HEADS * HEAD), 1.0, 6.0, ((0, 16), (1, 2)))
    out_weight = noise(splits[5], (HEADS * HEAD, D), (HEADS * HEAD) ** -0.5, 0.0625, ((0, 2), (1, 8)))
    decode_queries = draw_decode_queries(jax.random.fold_in(splits[14], 71), 0)
    decode_keys = draw_decode_keys(jax.random.fold_in(splits[14], 71), 0)
    decode_values = noise(splits[8], (ROWS, CTX_MAX, KV_HEADS * HEAD), 1.0, 6.0, ((0, 2), (1, 8), (2, 2)))
    new_keys = draw_new_keys(jax.random.fold_in(splits[14], 71), 0)
    new_values = noise(splits[10], (STEPS, ROWS, KV_HEADS * HEAD), 1.0, 6.0, ((1, 2), (2, 2)))
    request_lengths = set_ends(jax.random.randint(splits[11], (REQUESTS,), 1, CTX_MAX + 1), jax.random.fold_in(splits[11], 1), 1, CTX_MAX).astype(jnp.int32)
    row_requests = set_ends(jax.random.randint(splits[12], (ROWS,), 0, REQUESTS), jax.random.fold_in(splits[12], 1), 0, REQUESTS - 1).astype(jnp.int32)
    block_table_keys = jax.random.split(jax.random.fold_in(splits[13], 1), NBLOCKS // NBLOCKS)
    block_table_turns = jax.random.permutation(jax.random.fold_in(splits[13], 3), NBLOCKS // NBLOCKS)
    block_table = jax.vmap(lambda own, number: deal_out(jax.random.fold_in(splits[13], 2), own, number, NBLOCKS, OWNERS, 1, MOST, 2))(block_table_keys, block_table_turns).reshape((NBLOCKS, 1))
    return dict(prefill_queries=prefill_queries, cached_keys=cached_keys, cached_values=cached_values, span_keys=span_keys, span_values=span_values, out_weight=out_weight, decode_queries=decode_queries, decode_keys=decode_keys, decode_values=decode_values, new_keys=new_keys, new_values=new_values, request_lengths=request_lengths, row_requests=row_requests, block_table=block_table)


masked_score = -1.0e30


def reference(prefill_queries, cached_keys, cached_values, span_keys, span_values, out_weight, decode_queries, decode_keys, decode_values, new_keys, new_values, request_lengths, row_requests, block_table):
    score_scale = HEAD ** -0.5
    group_size = HEADS // KV_HEADS
    key_rows = jnp.concatenate([cached_keys, span_keys], axis=0).reshape(CONTEXT + SPAN, KV_HEADS, HEAD)
    value_rows = jnp.concatenate([cached_values, span_values], axis=0).reshape(CONTEXT + SPAN, KV_HEADS, HEAD)
    query_index = jnp.arange(SPAN, dtype=jnp.int32)
    key_index = jnp.arange(CONTEXT + SPAN, dtype=jnp.int32) - CONTEXT
    visible = key_index[None, :] <= query_index[:, None]
    queries = prefill_queries.reshape(SPAN, HEADS, HEAD).transpose(1, 0, 2)

    def one_head(inputs):
        query_rows, head_number = inputs
        keys_one = lax.dynamic_index_in_dim(key_rows, head_number // group_size, 1, keepdims=False)
        values_one = lax.dynamic_index_in_dim(value_rows, head_number // group_size, 1, keepdims=False)
        scores = jnp.einsum("qd,kd->qk", query_rows, keys_one, preferred_element_type=jnp.float32) * score_scale
        scores = jnp.where(visible, scores, masked_score)
        row_peak = jnp.max(scores, axis=1)
        weights = jnp.where(visible, jnp.exp(scores - row_peak[:, None]), 0.0)
        totals = jnp.sum(weights, axis=1)
        weighted = jnp.dot(weights.astype(jnp.bfloat16), values_one, preferred_element_type=jnp.float32)
        return (weighted / totals[:, None]).astype(jnp.bfloat16)

    attention = lax.map(one_head, (queries, jnp.arange(HEADS, dtype=jnp.int32)))
    attention = attention.transpose(1, 0, 2).reshape(SPAN, HEADS * HEAD)
    prefill_out = jnp.dot(attention, out_weight, preferred_element_type=jnp.float32).astype(jnp.bfloat16)

    dec_queries = decode_queries.astype(jnp.float32).reshape(STEPS, ROWS, KV_HEADS, group_size, HEAD)
    dec_keys = decode_keys.astype(jnp.float32).reshape(ROWS, CTX_MAX, KV_HEADS, HEAD)
    dec_values = decode_values.astype(jnp.float32).reshape(ROWS, CTX_MAX, KV_HEADS, HEAD)
    step_keys = new_keys.astype(jnp.float32).reshape(STEPS, ROWS, KV_HEADS, HEAD)
    step_values = new_values.astype(jnp.float32).reshape(STEPS, ROWS, KV_HEADS, HEAD)
    row_length = request_lengths[row_requests]
    live = jnp.arange(CTX_MAX, dtype=jnp.int32)[None, :] < row_length[:, None]
    causal = jnp.arange(STEPS, dtype=jnp.int32)[None, :] <= jnp.arange(STEPS, dtype=jnp.int32)[:, None]

    def one_group(kv_number):
        query_part = lax.dynamic_index_in_dim(dec_queries, kv_number, 2, keepdims=False)
        keys_part = lax.dynamic_index_in_dim(dec_keys, kv_number, 2, keepdims=False)
        values_part = lax.dynamic_index_in_dim(dec_values, kv_number, 2, keepdims=False)
        step_key_part = lax.dynamic_index_in_dim(step_keys, kv_number, 2, keepdims=False)
        step_value_part = lax.dynamic_index_in_dim(step_values, kv_number, 2, keepdims=False)
        cache_scores = jnp.einsum("trgd,rsd->rgts", query_part, keys_part) * score_scale
        cache_scores = jnp.where(live[:, None, None, :], cache_scores, masked_score)
        step_scores = jnp.einsum("trgd,urd->rgtu", query_part, step_key_part) * score_scale
        step_scores = jnp.where(causal, step_scores, masked_score)
        peak = jnp.maximum(jnp.max(cache_scores, axis=3), jnp.max(step_scores, axis=3))
        cache_weights = jnp.where(live[:, None, None, :], jnp.exp(cache_scores - peak[..., None]), 0.0)
        step_weights = jnp.where(causal, jnp.exp(step_scores - peak[..., None]), 0.0)
        totals = jnp.sum(cache_weights, axis=3) + jnp.sum(step_weights, axis=3)
        weighted = jnp.einsum("rgts,rsd->rgtd", cache_weights.astype(jnp.bfloat16).astype(jnp.float32), values_part)
        weighted = weighted + jnp.einsum("rgtu,urd->rgtd", step_weights.astype(jnp.bfloat16).astype(jnp.float32), step_value_part)
        return (weighted / totals[..., None]).astype(jnp.bfloat16)

    decoded = lax.map(one_group, jnp.arange(KV_HEADS, dtype=jnp.int32))
    decoded = decoded.transpose(3, 1, 0, 2, 4).reshape(STEPS * ROWS, HEADS * HEAD)
    decode_out = jnp.dot(decoded, out_weight, preferred_element_type=jnp.float32).astype(jnp.bfloat16).reshape(STEPS, ROWS, D)

    targets = block_table[:, 0]
    block_order = jnp.arange(NBLOCKS, dtype=jnp.int32)
    earlier = (targets[None, :] == targets[:, None]) & (block_order[None, :] < block_order[:, None])
    block_rank = jnp.sum(earlier.astype(jnp.int32), axis=1)
    owner_ids = jnp.arange(OWNERS, dtype=jnp.int32)
    slot_ids = jnp.arange(MOST, dtype=jnp.int32)
    chosen = (targets[None, None, :] == owner_ids[:, None, None]) & (block_rank[None, None, :] == slot_ids[None, :, None])
    chosen = chosen.astype(jnp.float32).reshape(OWNERS * MOST, NBLOCKS)
    key_blocks = span_keys.astype(jnp.float32).reshape(NBLOCKS, BLOCK * KV_HEADS * HEAD)
    value_blocks = span_values.astype(jnp.float32).reshape(NBLOCKS, BLOCK * KV_HEADS * HEAD)
    landed_keys = jnp.dot(chosen, key_blocks).astype(jnp.bfloat16).reshape(OWNERS, MOST, BLOCK, KV_HEADS * HEAD)
    landed_values = jnp.dot(chosen, value_blocks).astype(jnp.bfloat16).reshape(OWNERS, MOST, BLOCK, KV_HEADS * HEAD)
    return (prefill_out, decode_out, landed_keys, landed_values)
```

```python
import functools
import math

import jax
import jax.numpy as jnp
from jax import lax
from jax.experimental import pallas as pl
from jax.experimental.pallas import tpu as pltpu
from jax.sharding import PartitionSpec as P

HEADS = 64
KV_HEADS = 8
HEAD = 128
BLOCK = 4
LANES = 128
SCALE = HEAD ** (-0.5)
SCALE2 = SCALE * math.log2(math.e)
masked_score = -1e30
MESH = pl.DeviceIdType.MESH
VMEM_LIMIT = 56 * 1024 * 1024


def dot_t(a, b):
    return lax.dot_general(a, b, (((1,), (1,)), ((), ())), preferred_element_type=jnp.float32)


def prefill_kernel(
    group_size, chunk, first_ref, q_ref, k_ref, v_ref, sk_ref, sv_ref, o_ref, lse_ref, va, sva
):
    step = pl.program_id(0)
    rows = q_ref.shape[0]
    span = sk_ref.shape[0]
    va[:, :HEAD] = v_ref[...]
    va[:, HEAD:] = jnp.ones((va.shape[0], HEAD), jnp.bfloat16)
    sva[:, :HEAD] = sv_ref[...]
    sva[:, HEAD:] = jnp.ones((span, HEAD), jnp.bfloat16)

    @pl.when(step == 0)
    def _():
        lse_ref[...] = jnp.zeros_like(lse_ref)

    first = first_ref[0]
    lane = lax.broadcasted_iota(jnp.int32, (chunk, LANES), 1)
    for head in range(group_size):
        columns = slice(head * HEAD, (head + 1) * HEAD)
        for start in range(0, rows, chunk):
            here = slice(start, start + chunk)
            q = q_ref[here, columns]
            s = dot_t(q, k_ref[...])
            t = dot_t(q, sk_ref[...])
            key = first + lax.broadcasted_iota(jnp.int32, (chunk, span), 1)
            query = start + lax.broadcasted_iota(jnp.int32, (chunk, span), 0)
            t = jnp.where(key <= query, t, masked_score)
            top = jnp.maximum(
                jnp.max(s, axis=1, keepdims=True), jnp.max(t, axis=1, keepdims=True)
            )
            shift = top * SCALE2
            p = jnp.exp2(s * SCALE2 - shift).astype(jnp.bfloat16)
            u = jnp.exp2(t * SCALE2 - shift).astype(jnp.bfloat16)
            acc = jnp.dot(p, va[...], preferred_element_type=jnp.float32)
            acc = acc + jnp.dot(u, sva[...], preferred_element_type=jnp.float32)
            total = acc[:, HEAD:]
            o_ref[here, columns] = (acc[:, :HEAD] / total).astype(jnp.bfloat16)
            lse = top * SCALE + jnp.log(total)
            lse_ref[here, :] = jnp.where(lane == step * group_size + head, lse, lse_ref[here, :])


def prefill_local(first, q, keys, values, span_keys, span_values):
    rows, width = q.shape
    local_groups = keys.shape[1] // HEAD
    group_size = HEADS // KV_HEADS
    chunk = min(256, rows)
    wide = group_size * HEAD
    by_group = lambda i: (0, i)
    return pl.pallas_call(
        functools.partial(prefill_kernel, group_size, chunk),
        grid=(local_groups,),
        out_shape=(
            jax.ShapeDtypeStruct((rows, width), jnp.bfloat16),
            jax.ShapeDtypeStruct((rows, LANES), jnp.float32),
        ),
        in_specs=[
            pl.BlockSpec(memory_space=pltpu.SMEM),
            pl.BlockSpec((rows, wide), by_group),
            pl.BlockSpec((keys.shape[0], HEAD), by_group),
            pl.BlockSpec((keys.shape[0], HEAD), by_group),
            pl.BlockSpec((span_keys.shape[0], HEAD), by_group),
            pl.BlockSpec((span_keys.shape[0], HEAD), by_group),
        ],
        out_specs=(
            pl.BlockSpec((rows, wide), by_group),
            pl.BlockSpec((rows, LANES), lambda i: (0, 0)),
        ),
        scratch_shapes=[
            pltpu.VMEM((keys.shape[0], 2 * HEAD), jnp.bfloat16),
            pltpu.VMEM((span_keys.shape[0], 2 * HEAD), jnp.bfloat16),
        ],
        compiler_params=pltpu.CompilerParams(vmem_limit_bytes=VMEM_LIMIT),
        cost_estimate=pl.CostEstimate(
            flops=4 * rows * width * keys.shape[0],
            bytes_accessed=4 * rows * width + 4 * keys.size,
            transcendentals=rows * width // HEAD * keys.shape[0],
        ),
    )(first, q, keys, values, span_keys, span_values)


def decode_kernel(
    group_size, length_ref, where_ref, q_ref, k_ref, v_ref, nk_ref, nv_ref, o_ref, lse_ref
):
    row = pl.program_id(0)
    slots = k_ref.shape[1]
    local_groups, many = q_ref.shape[1], q_ref.shape[2]
    steps = nk_ref.shape[2]
    length = length_ref[row] - where_ref[0] * slots
    live = lax.broadcasted_iota(jnp.int32, (many, slots), 1) < length
    query_step = lax.broadcasted_iota(jnp.int32, (many, steps), 0) // group_size
    token = lax.broadcasted_iota(jnp.int32, (many, steps), 1)
    seen = (token <= query_step) & (where_ref[0] == 0)
    for group in range(local_groups):
        columns = slice(group * HEAD, (group + 1) * HEAD)
        q = q_ref[0, group]
        s = jnp.where(live, dot_t(q, k_ref[0, :, columns]), masked_score)
        t = jnp.where(seen, dot_t(q, nk_ref[0, group]), masked_score)
        top = jnp.maximum(jnp.max(s, axis=1, keepdims=True), jnp.max(t, axis=1, keepdims=True))
        shift = top * SCALE2
        p = jnp.where(live, jnp.exp2(s * SCALE2 - shift), 0.0)
        u = jnp.where(seen, jnp.exp2(t * SCALE2 - shift), 0.0)
        total = jnp.sum(p, axis=1, keepdims=True) + jnp.sum(u, axis=1, keepdims=True)
        acc = jnp.dot(
            p.astype(jnp.bfloat16), v_ref[0, :, columns], preferred_element_type=jnp.float32
        )
        acc = acc + jnp.dot(
            u.astype(jnp.bfloat16), nv_ref[0, group], preferred_element_type=jnp.float32
        )
        any_key = total > 0.0
        safe = jnp.where(any_key, total, 1.0)
        o_ref[0, group] = (acc / safe).astype(jnp.bfloat16)
        lse = jnp.where(any_key, top * SCALE + jnp.log(safe), masked_score)
        lse_ref[0, group] = jnp.broadcast_to(lse, (many, LANES))


def decode_local(lengths, where, q, keys, values, new_keys, new_values):
    rows, local_groups, many, _ = q.shape
    slots, width = keys.shape[1:]
    steps = new_keys.shape[2]
    row4 = lambda i: (i, 0, 0, 0)
    row3 = lambda i: (i, 0, 0)
    return pl.pallas_call(
        functools.partial(decode_kernel, HEADS // KV_HEADS),
        grid=(rows,),
        out_shape=(
            jax.ShapeDtypeStruct(q.shape, jnp.bfloat16),
            jax.ShapeDtypeStruct((rows, local_groups, many, LANES), jnp.float32),
        ),
        in_specs=[
            pl.BlockSpec(memory_space=pltpu.SMEM),
            pl.BlockSpec(memory_space=pltpu.SMEM),
            pl.BlockSpec((1, local_groups, many, HEAD), row4),
            pl.BlockSpec((1, slots, width), row3),
            pl.BlockSpec((1, slots, width), row3),
            pl.BlockSpec((1, local_groups, steps, HEAD), row4),
            pl.BlockSpec((1, local_groups, steps, HEAD), row4),
        ],
        out_specs=(
            pl.BlockSpec((1, local_groups, many, HEAD), row4),
            pl.BlockSpec((1, local_groups, many, LANES), row4),
        ),
        compiler_params=pltpu.CompilerParams(vmem_limit_bytes=VMEM_LIMIT),
        cost_estimate=pl.CostEstimate(
            flops=4 * rows * many * slots * width,
            bytes_accessed=4 * keys.size,
            transcendentals=rows * local_groups * many * slots,
        ),
    )(lengths, where, q, keys, values, new_keys, new_values)


def merge_kernel(
    n, heads, o_ref, l_ref, od_ref, ld_ref, out_ref,
    xo, xl, cb, cl, rb, rl,
    xo_send, xo_recv, xl_send, xl_recv, ro_send, ro_recv, rl_send, rl_recv, g_send, g_recv,
):
    me = lax.axis_index("seq")
    mine = lax.axis_index("group")
    other = 1 - mine

    barrier = pltpu.get_barrier_semaphore()
    pl.semaphore_signal(barrier, inc=1, device_id={"group": other}, device_id_type=MESH)
    for k in range(1, n):
        pl.semaphore_signal(
            barrier, inc=1, device_id={"seq": lax.rem(me + k, n)}, device_id_type=MESH
        )
    pl.semaphore_wait(barrier, n)

    def chip_copies(k):
        s = lax.rem(me + 1 + k, n)
        return (
            pltpu.make_async_remote_copy(
                src_ref=o_ref.at[other, s], dst_ref=xo.at[s],
                send_sem=xo_send.at[k], recv_sem=xo_recv.at[k],
                device_id={"group": other}, device_id_type=MESH,
            ),
            pltpu.make_async_remote_copy(
                src_ref=l_ref.at[other, s], dst_ref=xl.at[s],
                send_sem=xl_send.at[k], recv_sem=xl_recv.at[k],
                device_id={"group": other}, device_id_type=MESH,
            ),
        )

    def seq_copies(k):
        s = lax.rem(me + 1 + k, n)
        return (
            pltpu.make_async_remote_copy(
                src_ref=cb.at[s], dst_ref=rb.at[k],
                send_sem=ro_send.at[k], recv_sem=ro_recv.at[k],
                device_id={"seq": s}, device_id_type=MESH,
            ),
            pltpu.make_async_remote_copy(
                src_ref=cl.at[s], dst_ref=rl.at[k],
                send_sem=rl_send.at[k], recv_sem=rl_recv.at[k],
                device_id={"seq": s}, device_id_type=MESH,
            ),
        )

    def gather_copy(k):
        return pltpu.make_async_remote_copy(
            src_ref=out_ref.at[me], dst_ref=out_ref.at[me],
            send_sem=g_send.at[k], recv_sem=g_recv.at[k],
            device_id={"seq": lax.rem(me + 1 + k, n)}, device_id_type=MESH,
        )

    def start_chip(k, carry):
        for copy in chip_copies(k):
            copy.start()
        return carry

    lax.fori_loop(0, n, start_chip, 0)

    def merge_pair(k):
        s = lax.rem(me + 1 + k, n)
        for copy in chip_copies(k):
            copy.wait_recv()
        la, lb = l_ref[mine, s], xl[s]
        top = jnp.maximum(la, lb)
        wa, wb = jnp.exp(la - top), jnp.exp(lb - top)
        total = wa + wb
        wa, wb = wa / total, wb / total
        cl[s] = jnp.concatenate([top + jnp.log(total), ld_ref[s]], axis=0)
        for head in range(heads):
            columns = slice(head * HEAD, (head + 1) * HEAD)
            both = (
                o_ref[mine, s, :, columns].astype(jnp.float32) * wa[:, head : head + 1]
                + xo[s, :, columns].astype(jnp.float32) * wb[:, head : head + 1]
            )
            both = jnp.concatenate([both, od_ref[s, :, columns].astype(jnp.float32)], axis=0)
            cb[s, :, columns] = both.astype(jnp.bfloat16)

    def pair_and_send(k, carry):
        merge_pair(k)
        for copy in seq_copies(k):
            copy.start()
        return carry

    lax.fori_loop(0, n - 1, pair_and_send, 0)
    merge_pair(n - 1)

    def wait_seq(k, carry):
        for copy in seq_copies(k):
            copy.wait_recv()
        return carry

    lax.fori_loop(0, n - 1, wait_seq, 0)
    logs = [cl[me]] + [rl[k] for k in range(n - 1)]
    top = functools.reduce(jnp.maximum, logs)
    weights = [jnp.exp(one - top) for one in logs]
    total = functools.reduce(jnp.add, weights)
    weights = [one / total for one in weights]
    for head in range(heads):
        columns = slice(head * HEAD, (head + 1) * HEAD)
        one_column = slice(head, head + 1)
        total = cb[me, :, columns].astype(jnp.float32) * weights[0][:, one_column]
        for k in range(n - 1):
            total = total + rb[k, :, columns].astype(jnp.float32) * weights[k + 1][:, one_column]
        out_ref[me, :, columns] = total.astype(jnp.bfloat16)

    def start_gather(k, carry):
        gather_copy(k).start()
        return carry

    lax.fori_loop(0, n - 1, start_gather, 0)

    def finish_chip(k, carry):
        for copy in chip_copies(k):
            copy.wait_send()
        return carry

    lax.fori_loop(0, n, finish_chip, 0)

    def finish(k, carry):
        for copy in seq_copies(k):
            copy.wait_send()
        gather_copy(k).wait()
        return carry

    lax.fori_loop(0, n - 1, finish, 0)


def merge(n, o, lse, od, lsed):
    _, _, span_block, width = o.shape
    rows = span_block + od.shape[1]
    vmem = pl.BlockSpec(memory_space=pltpu.VMEM)
    return pl.pallas_call(
        functools.partial(merge_kernel, n, width // HEAD),
        out_shape=jax.ShapeDtypeStruct((n, rows, width), jnp.bfloat16),
        in_specs=[vmem] * 4,
        out_specs=vmem,
        scratch_shapes=[
            pltpu.VMEM((n, span_block, width), jnp.bfloat16),
            pltpu.VMEM((n, span_block, LANES), jnp.float32),
            pltpu.VMEM((n, rows, width), jnp.bfloat16),
            pltpu.VMEM((n, rows, LANES), jnp.float32),
            pltpu.VMEM((n - 1, rows, width), jnp.bfloat16),
            pltpu.VMEM((n - 1, rows, LANES), jnp.float32),
        ]
        + [pltpu.SemaphoreType.DMA((n,))] * 10,
        compiler_params=pltpu.CompilerParams(
            collective_id=0, has_side_effects=True, vmem_limit_bytes=VMEM_LIMIT
        ),
    )(o, lse, od, lsed)


def body(
    prefill_queries,
    cached_keys,
    cached_values,
    span_keys,
    span_values,
    out_weight,
    decode_queries,
    decode_keys,
    decode_values,
    new_keys,
    new_values,
    request_lengths,
    row_requests,
    block_table,
):
    seq_count = lax.axis_size("seq")
    group_count = lax.axis_size("group")
    seq_index = lax.axis_index("seq")
    owner_index = seq_index * group_count + lax.axis_index("group")
    group_size = HEADS // KV_HEADS
    span_rows, width = prefill_queries.shape
    local_heads = width // HEAD
    local_groups = cached_keys.shape[1] // HEAD
    span_local = span_keys.shape[0]
    span_block = span_rows // (seq_count * group_count)

    both = jnp.concatenate([span_keys, span_values], axis=1)
    gathered = lax.all_gather(both, ("seq", "group"), axis=0, tiled=True)

    first = (owner_index * span_local).astype(jnp.int32).reshape(1)
    o, lse = prefill_local(
        first, prefill_queries, cached_keys, cached_values, span_keys, span_values
    )
    o = o.reshape(group_count, seq_count, span_block, width)
    lse = lse.reshape(group_count, seq_count, span_block, LANES)

    steps, rows_local = decode_queries.shape[:2]
    decode_rows = steps * rows_local
    step_queries = decode_queries.reshape(steps, rows_local, local_groups, group_size, HEAD)
    step_queries = step_queries.transpose(1, 2, 0, 3, 4).reshape(
        rows_local, local_groups, steps * group_size, HEAD
    )
    by_row = lambda x: x.reshape(steps, rows_local, local_groups, HEAD).transpose(1, 2, 0, 3)
    picked = (
        row_requests[:, None] == jnp.arange(request_lengths.shape[0], dtype=jnp.int32)[None, :]
    )
    row_length = jnp.sum(jnp.where(picked, request_lengths[None, :], 0), axis=1)
    od, lsed = decode_local(
        row_length.astype(jnp.int32),
        seq_index.astype(jnp.int32).reshape(1),
        step_queries,
        decode_keys,
        decode_values,
        by_row(new_keys),
        by_row(new_values),
    )
    decode_block = decode_rows // seq_count
    od = od.reshape(rows_local, local_groups, steps, group_size, HEAD)
    od = od.transpose(2, 0, 1, 3, 4).reshape(seq_count, decode_block, width)
    lsed = lsed[..., 0].reshape(rows_local, local_groups, steps, group_size)
    lsed = lsed.transpose(2, 0, 1, 3).reshape(decode_rows, local_heads)
    lsed = jnp.pad(lsed, ((0, 0), (0, LANES - local_heads)))
    lsed = lsed.reshape(seq_count, decode_block, LANES)

    attention = merge(seq_count, o, lse, od, lsed)
    attention = attention.reshape(seq_count * (span_block + decode_block), width)
    partial = jnp.dot(attention, out_weight, preferred_element_type=jnp.float32)
    part = lax.psum_scatter(partial, "tensor", scatter_dimension=1, tiled=True)
    part = part.astype(jnp.bfloat16).reshape(seq_count, span_block + decode_block, -1)
    prefill_out = part[:, :span_block].reshape(seq_count * span_block, -1)
    decode_out = part[:, span_block:].reshape(steps, rows_local, -1)

    block_count = span_rows // BLOCK
    most_blocks = 2 * block_count // (seq_count * group_count)
    targets = block_table[:, 0]
    block_order = jnp.arange(block_count, dtype=jnp.int32)
    earlier = (targets[None, :] == targets[:, None]) & (block_order[None, :] < block_order[:, None])
    block_rank = jnp.sum(earlier.astype(jnp.int32), axis=1)
    slot_ids = jnp.arange(most_blocks, dtype=jnp.int32)
    chosen = (targets[None, :] == owner_index) & (block_rank[None, :] == slot_ids[:, None])
    chosen = chosen.astype(jnp.bfloat16)
    landed = jnp.dot(
        chosen, gathered.reshape(block_count, -1), preferred_element_type=jnp.float32
    ).astype(jnp.bfloat16)
    landed = landed.reshape(1, most_blocks, BLOCK, 2, -1)
    return (prefill_out, decode_out, landed[:, :, :, 0], landed[:, :, :, 1])


def solution(mesh):
    placed = (
        P(None, "tensor"),
        P(("seq", "group"), "tensor"),
        P(("seq", "group"), "tensor"),
        P(("seq", "group"), "tensor"),
        P(("seq", "group"), "tensor"),
        P("tensor", "seq"),
        P(None, "group", "tensor"),
        P("group", "seq", "tensor"),
        P("group", "seq", "tensor"),
        P(None, "group", "tensor"),
        P(None, "group", "tensor"),
        P(),
        P("group"),
        P(),
    )
    return jax.shard_map(
        body,
        mesh=mesh,
        in_specs=placed,
        out_specs=(
            P("group", ("seq", "tensor")),
            P(None, "group", ("seq", "tensor")),
            P(("seq", "group"), None, None, "tensor"),
            P(("seq", "group"), None, None, "tensor"),
        ),
        check_vma=False,
    )
```

```python
import functools
import math

import jax
import jax.numpy as jnp
from jax import lax
from jax.experimental import pallas as pl
from jax.experimental.pallas import tpu as pltpu
from jax.sharding import PartitionSpec as P

HEADS = 64
KV_HEADS = 8
HEAD = 128
BLOCK = 4
LANES = 128
SCALE = HEAD ** (-0.5)
SCALE2 = SCALE * math.log2(math.e)
masked_score = -1e30
MESH = pl.DeviceIdType.MESH
VMEM_LIMIT = 56 * 1024 * 1024


def dot_t(a, b):
    return lax.dot_general(a, b, (((1,), (1,)), ((), ())), preferred_element_type=jnp.float32)


def prefill_kernel(
    group_size, chunk, first_ref, q_ref, k_ref, v_ref, sk_ref, sv_ref, o_ref, lse_ref, va, sva
):
    step = pl.program_id(0)
    rows = q_ref.shape[0]
    span = sk_ref.shape[0]
    va[:, :HEAD] = v_ref[...]
    va[:, HEAD:] = jnp.ones((va.shape[0], HEAD), jnp.bfloat16)
    sva[:, :HEAD] = sv_ref[...]
    sva[:, HEAD:] = jnp.ones((span, HEAD), jnp.bfloat16)

    @pl.when(step == 0)
    def _():
        lse_ref[...] = jnp.zeros_like(lse_ref)

    first = first_ref[0]
    lane = lax.broadcasted_iota(jnp.int32, (chunk, LANES), 1)
    for head in range(group_size):
        columns = slice(head * HEAD, (head + 1) * HEAD)
        for start in range(0, rows, chunk):
            here = slice(start, start + chunk)
            q = q_ref[here, columns]
            s = dot_t(q, k_ref[...])
            t = dot_t(q, sk_ref[...])
            key = first + lax.broadcasted_iota(jnp.int32, (chunk, span), 1)
            query = start + lax.broadcasted_iota(jnp.int32, (chunk, span), 0)
            t = jnp.where(key <= query, t, masked_score)
            top = jnp.maximum(
                jnp.max(s, axis=1, keepdims=True), jnp.max(t, axis=1, keepdims=True)
            )
            shift = top * SCALE2
            p = jnp.exp2(s * SCALE2 - shift).astype(jnp.bfloat16)
            u = jnp.exp2(t * SCALE2 - shift).astype(jnp.bfloat16)
            acc = jnp.dot(p, va[...], preferred_element_type=jnp.float32)
            acc = acc + jnp.dot(u, sva[...], preferred_element_type=jnp.float32)
            total = acc[:, HEAD:]
            o_ref[here, columns] = (acc[:, :HEAD] / total).astype(jnp.bfloat16)
            lse = top * SCALE + jnp.log(total)
            lse_ref[here, :] = jnp.where(lane == step * group_size + head, lse, lse_ref[here, :])


def prefill_local(first, q, keys, values, span_keys, span_values):
    rows, width = q.shape
    local_groups = keys.shape[1] // HEAD
    group_size = HEADS // KV_HEADS
    chunk = min(256, rows)
    wide = group_size * HEAD
    by_group = lambda i: (0, i)
    return pl.pallas_call(
        functools.partial(prefill_kernel, group_size, chunk),
        grid=(local_groups,),
        out_shape=(
            jax.ShapeDtypeStruct((rows, width), jnp.bfloat16),
            jax.ShapeDtypeStruct((rows, LANES), jnp.float32),
        ),
        in_specs=[
            pl.BlockSpec(memory_space=pltpu.SMEM),
            pl.BlockSpec((rows, wide), by_group),
            pl.BlockSpec((keys.shape[0], HEAD), by_group),
            pl.BlockSpec((keys.shape[0], HEAD), by_group),
            pl.BlockSpec((span_keys.shape[0], HEAD), by_group),
            pl.BlockSpec((span_keys.shape[0], HEAD), by_group),
        ],
        out_specs=(
            pl.BlockSpec((rows, wide), by_group),
            pl.BlockSpec((rows, LANES), lambda i: (0, 0)),
        ),
        scratch_shapes=[
            pltpu.VMEM((keys.shape[0], 2 * HEAD), jnp.bfloat16),
            pltpu.VMEM((span_keys.shape[0], 2 * HEAD), jnp.bfloat16),
        ],
        compiler_params=pltpu.CompilerParams(vmem_limit_bytes=VMEM_LIMIT),
        cost_estimate=pl.CostEstimate(
            flops=4 * rows * width * keys.shape[0],
            bytes_accessed=4 * rows * width + 4 * keys.size,
            transcendentals=rows * width // HEAD * keys.shape[0],
        ),
    )(first, q, keys, values, span_keys, span_values)


def decode_kernel(
    group_size, length_ref, where_ref, q_ref, k_ref, v_ref, nk_ref, nv_ref, o_ref, lse_ref
):
    row = pl.program_id(0)
    slots = k_ref.shape[1]
    local_groups, many = q_ref.shape[1], q_ref.shape[2]
    steps = nk_ref.shape[2]
    length = length_ref[row] - where_ref[0] * slots
    live = lax.broadcasted_iota(jnp.int32, (many, slots), 1) < length
    query_step = lax.broadcasted_iota(jnp.int32, (many, steps), 0) // group_size
    token = lax.broadcasted_iota(jnp.int32, (many, steps), 1)
    seen = (token <= query_step) & (where_ref[0] == 0)
    columns = [slice(group * HEAD, (group + 1) * HEAD) for group in range(local_groups)]
    groups = range(local_groups)
    stack = lambda parts: jnp.concatenate(parts, axis=0)
    s = stack([jnp.where(live, dot_t(q_ref[0, g], k_ref[0, :, columns[g]]), masked_score) for g in groups])
    t = stack([jnp.where(seen, dot_t(q_ref[0, g], nk_ref[0, g]), masked_score) for g in groups])
    top = jnp.maximum(jnp.max(s, axis=1, keepdims=True), jnp.max(t, axis=1, keepdims=True))
    shift = top * SCALE2
    p = jnp.where(s > 0.5 * masked_score, jnp.exp2(s * SCALE2 - shift), 0.0)
    u = jnp.where(t > 0.5 * masked_score, jnp.exp2(t * SCALE2 - shift), 0.0)
    total = jnp.sum(p, axis=1, keepdims=True) + jnp.sum(u, axis=1, keepdims=True)
    any_key = total > 0.0
    safe = jnp.where(any_key, total, 1.0)
    lse = jnp.where(any_key, top * SCALE + jnp.log(safe), masked_score)
    lse = jnp.broadcast_to(lse, (local_groups * many, LANES))
    p, u, share = p.astype(jnp.bfloat16), u.astype(jnp.bfloat16), 1.0 / safe
    for g in groups:
        here = slice(g * many, (g + 1) * many)
        acc = jnp.dot(p[here], v_ref[0, :, columns[g]], preferred_element_type=jnp.float32)
        acc = acc + jnp.dot(u[here], nv_ref[0, g], preferred_element_type=jnp.float32)
        o_ref[0, g] = (acc * share[here]).astype(jnp.bfloat16)
        lse_ref[0, g] = lse[here]


def decode_local(lengths, where, q, keys, values, new_keys, new_values):
    rows, local_groups, many, _ = q.shape
    slots, width = keys.shape[1:]
    steps = new_keys.shape[2]
    row4 = lambda i: (i, 0, 0, 0)
    row3 = lambda i: (i, 0, 0)
    return pl.pallas_call(
        functools.partial(decode_kernel, HEADS // KV_HEADS),
        grid=(rows,),
        out_shape=(
            jax.ShapeDtypeStruct(q.shape, jnp.bfloat16),
            jax.ShapeDtypeStruct((rows, local_groups, many, LANES), jnp.float32),
        ),
        in_specs=[
            pl.BlockSpec(memory_space=pltpu.SMEM),
            pl.BlockSpec(memory_space=pltpu.SMEM),
            pl.BlockSpec((1, local_groups, many, HEAD), row4),
            pl.BlockSpec((1, slots, width), row3),
            pl.BlockSpec((1, slots, width), row3),
            pl.BlockSpec((1, local_groups, steps, HEAD), row4),
            pl.BlockSpec((1, local_groups, steps, HEAD), row4),
        ],
        out_specs=(
            pl.BlockSpec((1, local_groups, many, HEAD), row4),
            pl.BlockSpec((1, local_groups, many, LANES), row4),
        ),
        compiler_params=pltpu.CompilerParams(vmem_limit_bytes=VMEM_LIMIT),
        cost_estimate=pl.CostEstimate(
            flops=4 * rows * many * slots * width,
            bytes_accessed=4 * keys.size,
            transcendentals=rows * local_groups * many * slots,
        ),
    )(lengths, where, q, keys, values, new_keys, new_values)


def merge_kernel(
    n, heads, o_ref, l_ref, od_ref, ld_ref, out_ref,
    xo, xl, cb, cl, co, yb, yl, zb, rb, rl,
    xo_send, xo_recv, xl_send, xl_recv, yo_send, yo_recv, yl_send, yl_recv,
    ro_send, ro_recv, rl_send, rl_recv, g_send, g_recv, f_send, f_recv,
):
    me = lax.axis_index("seq")
    mine = lax.axis_index("group")
    other = 1 - mine
    nz = n // 2
    z, y = me // 2, lax.rem(me, 2)
    beside = z * 2 + 1 - y

    def ahead(k):
        return lax.rem(z + 1 + k, nz)

    barrier = pltpu.get_barrier_semaphore()
    pl.semaphore_signal(barrier, inc=1, device_id={"group": other}, device_id_type=MESH)
    pl.semaphore_signal(barrier, inc=1, device_id={"seq": beside}, device_id_type=MESH)
    for k in range(nz - 1):
        pl.semaphore_signal(
            barrier, inc=1, device_id={"seq": ahead(k) * 2 + y}, device_id_type=MESH
        )
    pl.semaphore_wait(barrier, nz + 1)

    def send(src, dst, sends, recvs, k, device):
        return pltpu.make_async_remote_copy(
            src_ref=src, dst_ref=dst, send_sem=sends.at[k], recv_sem=recvs.at[k],
            device_id=device, device_id_type=MESH,
        )

    def chip_copies(k, s):
        there = {"group": other}
        return (
            send(o_ref.at[other, s], xo.at[s], xo_send, xo_recv, k, there),
            send(l_ref.at[other, s], xl.at[s], xl_send, xl_recv, k, there),
        )

    def y_copies(k):
        there = {"seq": beside}
        return (
            send(cb.at[k], yb.at[k], yo_send, yo_recv, k, there),
            send(cl.at[k], yl.at[k], yl_send, yl_recv, k, there),
        )

    def z_copies(k):
        there = {"seq": ahead(k) * 2 + y}
        return (
            send(zb.at[k], rb.at[k], ro_send, ro_recv, k, there),
            send(cl.at[nz + k], rl.at[k], rl_send, rl_recv, k, there),
        )

    def far(k):
        return ahead(k) * 2 + 1 - y

    def near(k):
        return ahead(k) * 2 + y

    def start_chip(k, carry):
        for copy in chip_copies(k, far(k)):
            copy.start()
        return carry

    def start_chip_near(k, carry):
        for copy in chip_copies(nz + k, near(k)):
            copy.start()
        return carry

    lax.fori_loop(0, nz, start_chip, 0)
    lax.fori_loop(0, nz, start_chip_near, 0)

    def pair_weights(la, lb):
        top = jnp.maximum(la, lb)
        wa, wb = jnp.exp(la - top), jnp.exp(lb - top)
        total = wa + wb
        return wa / total, wb / total, top + jnp.log(total)

    def merge_chip(k, slot, s, store):
        for copy in chip_copies(slot, s):
            copy.wait_recv()
        wa, wb, log = pair_weights(l_ref[mine, s], xl[s])
        cl[slot] = jnp.concatenate([log, ld_ref[s]], axis=0)
        for head in range(heads):
            columns = slice(head * HEAD, (head + 1) * HEAD)
            both = (
                o_ref[mine, s, :, columns].astype(jnp.float32) * wa[:, head : head + 1]
                + xo[s, :, columns].astype(jnp.float32) * wb[:, head : head + 1]
            )
            both = jnp.concatenate([both, od_ref[s, :, columns].astype(jnp.float32)], axis=0)
            store[k, :, columns] = both.astype(store.dtype)

    def phase_far(k, carry):
        merge_chip(k, k, far(k), cb)
        for copy in y_copies(k):
            copy.start()
        return carry

    def phase_near(k, carry):
        merge_chip(k, nz + k, near(k), co)
        return carry

    lax.fori_loop(0, nz, phase_far, 0)
    lax.fori_loop(0, nz, phase_near, 0)

    def merge_y(k):
        for copy in y_copies(k):
            copy.wait_recv()
        wa, wb, log = pair_weights(cl[nz + k], yl[k])
        cl[nz + k] = log
        for head in range(heads):
            columns = slice(head * HEAD, (head + 1) * HEAD)
            both = (
                co[k, :, columns] * wa[:, head : head + 1]
                + yb[k, :, columns].astype(jnp.float32) * wb[:, head : head + 1]
            )
            co[k, :, columns] = both
            zb[k, :, columns] = both.astype(jnp.bfloat16)

    def phase_y(k, carry):
        merge_y(k)
        for copy in z_copies(k):
            copy.start()
        return carry

    lax.fori_loop(0, nz - 1, phase_y, 0)
    merge_y(nz - 1)

    def wait_z(k, carry):
        for copy in z_copies(k):
            copy.wait_recv()
        return carry

    lax.fori_loop(0, nz - 1, wait_z, 0)
    logs = [cl[n - 1]] + [rl[k] for k in range(nz - 1)]
    top = functools.reduce(jnp.maximum, logs)
    weights = [jnp.exp(one - top) for one in logs]
    total = functools.reduce(jnp.add, weights)
    weights = [one / total for one in weights]
    for head in range(heads):
        columns = slice(head * HEAD, (head + 1) * HEAD)
        one_column = slice(head, head + 1)
        total = co[nz - 1, :, columns] * weights[0][:, one_column]
        for k in range(nz - 1):
            total = total + rb[k, :, columns].astype(jnp.float32) * weights[k + 1][:, one_column]
        out_ref[me, :, columns] = total.astype(jnp.bfloat16)

    def gather_z(k):
        return send(
            out_ref.at[me], out_ref.at[me], g_send, g_recv, k, {"seq": ahead(k) * 2 + y}
        )

    def forward(k):
        s = lax.rem(z - 1 - k + nz, nz) * 2 + y
        return send(out_ref.at[s], out_ref.at[s], f_send, f_recv, k, {"seq": beside})

    forward_own = send(out_ref.at[me], out_ref.at[me], f_send, f_recv, nz - 1, {"seq": beside})

    def start_gather(k, carry):
        gather_z(k).start()
        return carry

    forward_own.start()
    lax.fori_loop(0, nz - 1, start_gather, 0)

    def pass_on(k, carry):
        gather_z(k).wait_recv()
        forward(k).start()
        return carry

    lax.fori_loop(0, nz - 1, pass_on, 0)

    def finish(k, carry):
        for copy in chip_copies(k, far(k)) + chip_copies(nz + k, near(k)) + y_copies(k):
            copy.wait_send()
        return carry

    def finish_z(k, carry):
        for copy in z_copies(k):
            copy.wait_send()
        gather_z(k).wait_send()
        forward(k).wait()
        return carry

    lax.fori_loop(0, nz, finish, 0)
    lax.fori_loop(0, nz - 1, finish_z, 0)
    forward_own.wait()


def add_kernel(n, p_ref, out_ref, sb, rb, send_sem, recv_sem):
    me = lax.axis_index("tensor")
    barrier = pltpu.get_barrier_semaphore()
    for k in range(1, n):
        pl.semaphore_signal(
            barrier, inc=1, device_id={"tensor": lax.rem(me + k, n)}, device_id_type=MESH
        )
    pl.semaphore_wait(barrier, n - 1)

    def copy(k):
        return pltpu.make_async_remote_copy(
            src_ref=sb.at[k], dst_ref=rb.at[k], send_sem=send_sem.at[k], recv_sem=recv_sem.at[k],
            device_id={"tensor": lax.rem(me + 1 + k, n)}, device_id_type=MESH,
        )

    for k in range(n - 1):
        sb[k] = p_ref[lax.rem(me + 1 + k, n)].astype(jnp.bfloat16)
        copy(k).start()
    for k in range(n - 1):
        copy(k).wait_recv()
    total = p_ref[me]
    for k in range(n - 1):
        total = total + rb[k].astype(jnp.float32)
    out_ref[...] = total.astype(jnp.bfloat16)
    for k in range(n - 1):
        copy(k).wait_send()


def add_tensor(n, partial):
    _, rows, columns = partial.shape
    vmem = pl.BlockSpec(memory_space=pltpu.VMEM)
    return pl.pallas_call(
        functools.partial(add_kernel, n),
        out_shape=jax.ShapeDtypeStruct((rows, columns), jnp.bfloat16),
        in_specs=[vmem],
        out_specs=vmem,
        scratch_shapes=[
            pltpu.VMEM((n - 1, rows, columns), jnp.bfloat16),
            pltpu.VMEM((n - 1, rows, columns), jnp.bfloat16),
            pltpu.SemaphoreType.DMA((n - 1,)),
            pltpu.SemaphoreType.DMA((n - 1,)),
        ],
        compiler_params=pltpu.CompilerParams(
            collective_id=1, has_side_effects=True, vmem_limit_bytes=VMEM_LIMIT
        ),
    )(partial)


def merge(n, o, lse, od, lsed):
    _, _, span_block, width = o.shape
    rows = span_block + od.shape[1]
    vmem = pl.BlockSpec(memory_space=pltpu.VMEM)
    return pl.pallas_call(
        functools.partial(merge_kernel, n, width // HEAD),
        out_shape=jax.ShapeDtypeStruct((n, rows, width), jnp.bfloat16),
        in_specs=[vmem] * 4,
        out_specs=vmem,
        scratch_shapes=[
            pltpu.VMEM((n, span_block, width), jnp.bfloat16),
            pltpu.VMEM((n, span_block, LANES), jnp.float32),
            pltpu.VMEM((n // 2, rows, width), jnp.bfloat16),
            pltpu.VMEM((n, rows, LANES), jnp.float32),
            pltpu.VMEM((n // 2, rows, width), jnp.float32),
            pltpu.VMEM((n // 2, rows, width), jnp.bfloat16),
            pltpu.VMEM((n // 2, rows, LANES), jnp.float32),
            pltpu.VMEM((n // 2, rows, width), jnp.bfloat16),
            pltpu.VMEM((n // 2, rows, width), jnp.bfloat16),
            pltpu.VMEM((n // 2, rows, LANES), jnp.float32),
        ]
        + [pltpu.SemaphoreType.DMA((n,))] * 16,
        compiler_params=pltpu.CompilerParams(
            collective_id=0, has_side_effects=True, vmem_limit_bytes=VMEM_LIMIT
        ),
    )(o, lse, od, lsed)


def body(
    prefill_queries,
    cached_keys,
    cached_values,
    span_keys,
    span_values,
    out_weight,
    decode_queries,
    decode_keys,
    decode_values,
    new_keys,
    new_values,
    request_lengths,
    row_requests,
    block_table,
):
    seq_count = lax.axis_size("seq")
    group_count = lax.axis_size("group")
    seq_index = lax.axis_index("seq")
    owner_index = seq_index * group_count + lax.axis_index("group")
    group_size = HEADS // KV_HEADS
    span_rows, width = prefill_queries.shape
    local_heads = width // HEAD
    local_groups = cached_keys.shape[1] // HEAD
    span_local = span_keys.shape[0]
    span_block = span_rows // (seq_count * group_count)

    both = jnp.concatenate([span_keys, span_values], axis=1)
    gathered = lax.all_gather(both, ("seq", "group"), axis=0, tiled=True)

    first = (owner_index * span_local).astype(jnp.int32).reshape(1)
    o, lse = prefill_local(
        first, prefill_queries, cached_keys, cached_values, span_keys, span_values
    )
    o = o.reshape(group_count, seq_count, span_block, width)
    lse = lse.reshape(group_count, seq_count, span_block, LANES)

    steps, rows_local = decode_queries.shape[:2]
    decode_rows = steps * rows_local
    step_queries = decode_queries.reshape(steps, rows_local, local_groups, group_size, HEAD)
    step_queries = step_queries.transpose(1, 2, 0, 3, 4).reshape(
        rows_local, local_groups, steps * group_size, HEAD
    )
    by_row = lambda x: x.reshape(steps, rows_local, local_groups, HEAD).transpose(1, 2, 0, 3)
    picked = (
        row_requests[:, None] == jnp.arange(request_lengths.shape[0], dtype=jnp.int32)[None, :]
    )
    row_length = jnp.sum(jnp.where(picked, request_lengths[None, :], 0), axis=1)
    od, lsed = decode_local(
        row_length.astype(jnp.int32),
        seq_index.astype(jnp.int32).reshape(1),
        step_queries,
        decode_keys,
        decode_values,
        by_row(new_keys),
        by_row(new_values),
    )
    decode_block = decode_rows // seq_count
    od = od.reshape(rows_local, local_groups, steps, group_size, HEAD)
    od = od.transpose(2, 0, 1, 3, 4).reshape(seq_count, decode_block, width)
    lsed = lsed[..., 0].reshape(rows_local, local_groups, steps, group_size)
    lsed = lsed.transpose(2, 0, 1, 3).reshape(decode_rows, local_heads)
    lsed = jnp.pad(lsed, ((0, 0), (0, LANES - local_heads)))
    lsed = lsed.reshape(seq_count, decode_block, LANES)

    attention = merge(seq_count, o, lse, od, lsed)
    attention = attention.reshape(seq_count * (span_block + decode_block), width)
    partial = jnp.dot(attention, out_weight, preferred_element_type=jnp.float32)
    tensor_count = lax.axis_size("tensor")
    partial = partial.reshape(partial.shape[0], tensor_count, -1).transpose(1, 0, 2)
    part = add_tensor(tensor_count, partial).reshape(seq_count, span_block + decode_block, -1)
    prefill_out = part[:, :span_block].reshape(seq_count * span_block, -1)
    decode_out = part[:, span_block:].reshape(steps, rows_local, -1)

    block_count = span_rows // BLOCK
    most_blocks = 2 * block_count // (seq_count * group_count)
    targets = block_table[:, 0]
    block_order = jnp.arange(block_count, dtype=jnp.int32)
    earlier = (targets[None, :] == targets[:, None]) & (block_order[None, :] < block_order[:, None])
    block_rank = jnp.sum(earlier.astype(jnp.int32), axis=1)
    slot_ids = jnp.arange(most_blocks, dtype=jnp.int32)
    chosen = (targets[None, :] == owner_index) & (block_rank[None, :] == slot_ids[:, None])
    chosen = chosen.astype(jnp.bfloat16)
    landed = jnp.dot(
        chosen, gathered.reshape(block_count, -1), preferred_element_type=jnp.float32
    ).astype(jnp.bfloat16)
    landed = landed.reshape(1, most_blocks, BLOCK, 2, -1)
    return (prefill_out, decode_out, landed[:, :, :, 0], landed[:, :, :, 1])


def solution(mesh):
    placed = (
        P(None, "tensor"),
        P(("seq", "group"), "tensor"),
        P(("seq", "group"), "tensor"),
        P(("seq", "group"), "tensor"),
        P(("seq", "group"), "tensor"),
        P("tensor", "seq"),
        P(None, "group", "tensor"),
        P("group", "seq", "tensor"),
        P("group", "seq", "tensor"),
        P(None, "group", "tensor"),
        P(None, "group", "tensor"),
        P(),
        P("group"),
        P(),
    )
    return jax.shard_map(
        body,
        mesh=mesh,
        in_specs=placed,
        out_specs=(
            P("group", ("seq", "tensor")),
            P(None, "group", ("seq", "tensor")),
            P(("seq", "group"), None, None, "tensor"),
            P(("seq", "group"), None, None, "tensor"),
        ),
        check_vma=False,
    )
```

```python
import functools
import math

import jax
import jax.numpy as jnp
from jax import lax
from jax.experimental import pallas as pl
from jax.experimental.pallas import tpu as pltpu
from jax.sharding import PartitionSpec as P

HEADS = 64
KV_HEADS = 8
HEAD = 128
BLOCK = 4
LANES = 128
SCALE = HEAD ** (-0.5)
SCALE2 = SCALE * math.log2(math.e)
masked_score = -1e30
MESH = pl.DeviceIdType.MESH
VMEM_LIMIT = 56 * 1024 * 1024


def dot_t(a, b):
    return lax.dot_general(a, b, (((1,), (1,)), ((), ())), preferred_element_type=jnp.float32)


def prefill_kernel(
    group_size, chunk, first_ref, q_ref, k_ref, v_ref, sk_ref, sv_ref, o_ref, lse_ref, va, sva
):
    step = pl.program_id(0)
    rows = q_ref.shape[0]
    span = sk_ref.shape[0]
    va[:, :HEAD] = v_ref[...]
    va[:, HEAD:] = jnp.ones((va.shape[0], HEAD), jnp.bfloat16)
    sva[:, :HEAD] = sv_ref[...]
    sva[:, HEAD:] = jnp.ones((span, HEAD), jnp.bfloat16)

    @pl.when(step == 0)
    def _():
        lse_ref[...] = jnp.zeros_like(lse_ref)

    first = first_ref[0]
    lane = lax.broadcasted_iota(jnp.int32, (chunk, LANES), 1)
    for head in range(group_size):
        columns = slice(head * HEAD, (head + 1) * HEAD)
        for start in range(0, rows, chunk):
            here = slice(start, start + chunk)
            q = q_ref[here, columns]
            s = dot_t(q, k_ref[...])
            t = dot_t(q, sk_ref[...])
            key = first + lax.broadcasted_iota(jnp.int32, (chunk, span), 1)
            query = start + lax.broadcasted_iota(jnp.int32, (chunk, span), 0)
            t = jnp.where(key <= query, t, masked_score)
            top = jnp.maximum(
                jnp.max(s, axis=1, keepdims=True), jnp.max(t, axis=1, keepdims=True)
            )
            shift = top * SCALE2
            p = jnp.exp2(s * SCALE2 - shift).astype(jnp.bfloat16)
            u = jnp.exp2(t * SCALE2 - shift).astype(jnp.bfloat16)
            acc = jnp.dot(p, va[...], preferred_element_type=jnp.float32)
            acc = acc + jnp.dot(u, sva[...], preferred_element_type=jnp.float32)
            total = acc[:, HEAD:]
            o_ref[here, columns] = (acc[:, :HEAD] / total).astype(jnp.bfloat16)
            lse = top * SCALE + jnp.log(total)
            lse_ref[here, :] = jnp.where(lane == step * group_size + head, lse, lse_ref[here, :])


def prefill_local(first, q, keys, values, span_keys, span_values):
    rows, width = q.shape
    local_groups = keys.shape[1] // HEAD
    group_size = HEADS // KV_HEADS
    chunk = min(256, rows)
    wide = group_size * HEAD
    by_group = lambda i: (0, i)
    return pl.pallas_call(
        functools.partial(prefill_kernel, group_size, chunk),
        grid=(local_groups,),
        out_shape=(
            jax.ShapeDtypeStruct((rows, width), jnp.bfloat16),
            jax.ShapeDtypeStruct((rows, LANES), jnp.float32),
        ),
        in_specs=[
            pl.BlockSpec(memory_space=pltpu.SMEM),
            pl.BlockSpec((rows, wide), by_group),
            pl.BlockSpec((keys.shape[0], HEAD), by_group),
            pl.BlockSpec((keys.shape[0], HEAD), by_group),
            pl.BlockSpec((span_keys.shape[0], HEAD), by_group),
            pl.BlockSpec((span_keys.shape[0], HEAD), by_group),
        ],
        out_specs=(
            pl.BlockSpec((rows, wide), by_group),
            pl.BlockSpec((rows, LANES), lambda i: (0, 0)),
        ),
        scratch_shapes=[
            pltpu.VMEM((keys.shape[0], 2 * HEAD), jnp.bfloat16),
            pltpu.VMEM((span_keys.shape[0], 2 * HEAD), jnp.bfloat16),
        ],
        compiler_params=pltpu.CompilerParams(vmem_limit_bytes=VMEM_LIMIT),
        cost_estimate=pl.CostEstimate(
            flops=4 * rows * width * keys.shape[0],
            bytes_accessed=4 * rows * width + 4 * keys.size,
            transcendentals=rows * width // HEAD * keys.shape[0],
        ),
    )(first, q, keys, values, span_keys, span_values)


def decode_kernel(
    group_size, length_ref, where_ref, q_ref, k_ref, v_ref, nk_ref, nv_ref, o_ref, lse_ref
):
    row = pl.program_id(0)
    slots = k_ref.shape[1]
    local_groups, many = q_ref.shape[1], q_ref.shape[2]
    steps = nk_ref.shape[2]
    length = length_ref[row] - where_ref[0] * slots
    live = lax.broadcasted_iota(jnp.int32, (many, slots), 1) < length
    query_step = lax.broadcasted_iota(jnp.int32, (many, steps), 0) // group_size
    token = lax.broadcasted_iota(jnp.int32, (many, steps), 1)
    seen = (token <= query_step) & (where_ref[0] == 0)
    columns = [slice(group * HEAD, (group + 1) * HEAD) for group in range(local_groups)]
    groups = range(local_groups)
    stack = lambda parts: jnp.concatenate(parts, axis=0)
    s = stack([jnp.where(live, dot_t(q_ref[0, g], k_ref[0, :, columns[g]]), masked_score) for g in groups])
    t = stack([jnp.where(seen, dot_t(q_ref[0, g], nk_ref[0, g]), masked_score) for g in groups])
    top = jnp.maximum(jnp.max(s, axis=1, keepdims=True), jnp.max(t, axis=1, keepdims=True))
    shift = top * SCALE2
    p = jnp.where(s > 0.5 * masked_score, jnp.exp2(s * SCALE2 - shift), 0.0)
    u = jnp.where(t > 0.5 * masked_score, jnp.exp2(t * SCALE2 - shift), 0.0)
    total = jnp.sum(p, axis=1, keepdims=True) + jnp.sum(u, axis=1, keepdims=True)
    any_key = total > 0.0
    safe = jnp.where(any_key, total, 1.0)
    lse = jnp.where(any_key, top * SCALE + jnp.log(safe), masked_score)
    lse = jnp.broadcast_to(lse, (local_groups * many, LANES))
    p, u, share = p.astype(jnp.bfloat16), u.astype(jnp.bfloat16), 1.0 / safe
    for g in groups:
        here = slice(g * many, (g + 1) * many)
        acc = jnp.dot(p[here], v_ref[0, :, columns[g]], preferred_element_type=jnp.float32)
        acc = acc + jnp.dot(u[here], nv_ref[0, g], preferred_element_type=jnp.float32)
        o_ref[0, g] = (acc * share[here]).astype(jnp.bfloat16)
        lse_ref[0, g] = lse[here]


def decode_local(lengths, where, q, keys, values, new_keys, new_values):
    rows, local_groups, many, _ = q.shape
    slots, width = keys.shape[1:]
    steps = new_keys.shape[2]
    row4 = lambda i: (i, 0, 0, 0)
    row3 = lambda i: (i, 0, 0)
    return pl.pallas_call(
        functools.partial(decode_kernel, HEADS // KV_HEADS),
        grid=(rows,),
        out_shape=(
            jax.ShapeDtypeStruct(q.shape, jnp.bfloat16),
            jax.ShapeDtypeStruct((rows, local_groups, many, LANES), jnp.float32),
        ),
        in_specs=[
            pl.BlockSpec(memory_space=pltpu.SMEM),
            pl.BlockSpec(memory_space=pltpu.SMEM),
            pl.BlockSpec((1, local_groups, many, HEAD), row4),
            pl.BlockSpec((1, slots, width), row3),
            pl.BlockSpec((1, slots, width), row3),
            pl.BlockSpec((1, local_groups, steps, HEAD), row4),
            pl.BlockSpec((1, local_groups, steps, HEAD), row4),
        ],
        out_specs=(
            pl.BlockSpec((1, local_groups, many, HEAD), row4),
            pl.BlockSpec((1, local_groups, many, LANES), row4),
        ),
        compiler_params=pltpu.CompilerParams(vmem_limit_bytes=VMEM_LIMIT),
        cost_estimate=pl.CostEstimate(
            flops=4 * rows * many * slots * width,
            bytes_accessed=4 * keys.size,
            transcendentals=rows * local_groups * many * slots,
        ),
    )(lengths, where, q, keys, values, new_keys, new_values)


def merge_kernel(
    n, heads, o_ref, l_ref, od_ref, ld_ref, out_ref,
    xo, xl, cb, cl, co, yb, yl, zb, rb, rl,
    xo_send, xo_recv, xl_send, xl_recv, yo_send, yo_recv, yl_send, yl_recv,
    ro_send, ro_recv, rl_send, rl_recv, g_send, g_recv, f_send, f_recv,
):
    me = lax.axis_index("seq")
    mine = lax.axis_index("group")
    other = 1 - mine
    nz = n // 2
    z, y = me // 2, lax.rem(me, 2)
    beside = z * 2 + 1 - y

    def ahead(k):
        return lax.rem(z + 1 + k, nz)

    barrier = pltpu.get_barrier_semaphore()
    pl.semaphore_signal(barrier, inc=1, device_id={"group": other}, device_id_type=MESH)
    pl.semaphore_signal(barrier, inc=1, device_id={"seq": beside}, device_id_type=MESH)
    for k in range(nz - 1):
        pl.semaphore_signal(
            barrier, inc=1, device_id={"seq": ahead(k) * 2 + y}, device_id_type=MESH
        )
    pl.semaphore_wait(barrier, nz + 1)

    def send(src, dst, sends, recvs, k, device):
        return pltpu.make_async_remote_copy(
            src_ref=src, dst_ref=dst, send_sem=sends.at[k], recv_sem=recvs.at[k],
            device_id=device, device_id_type=MESH,
        )

    def chip_copies(k, s):
        there = {"group": other}
        return (
            send(o_ref.at[other, s], xo.at[s], xo_send, xo_recv, k, there),
            send(l_ref.at[other, s], xl.at[s], xl_send, xl_recv, k, there),
        )

    def y_copies(k):
        there = {"seq": beside}
        return (
            send(cb.at[k], yb.at[k], yo_send, yo_recv, k, there),
            send(cl.at[k], yl.at[k], yl_send, yl_recv, k, there),
        )

    def z_copies(k):
        there = {"seq": ahead(k) * 2 + y}
        return (
            send(zb.at[k], rb.at[k], ro_send, ro_recv, k, there),
            send(cl.at[nz + k], rl.at[k], rl_send, rl_recv, k, there),
        )

    def far(k):
        return ahead(k) * 2 + 1 - y

    def near(k):
        return ahead(k) * 2 + y

    def start_chip(k, carry):
        for copy in chip_copies(k, far(k)):
            copy.start()
        return carry

    def start_chip_near(k, carry):
        for copy in chip_copies(nz + k, near(k)):
            copy.start()
        return carry

    lax.fori_loop(0, nz, start_chip, 0)
    lax.fori_loop(0, nz, start_chip_near, 0)

    def pair_weights(la, lb):
        top = jnp.maximum(la, lb)
        wa, wb = jnp.exp(la - top), jnp.exp(lb - top)
        total = wa + wb
        return wa / total, wb / total, top + jnp.log(total)

    def merge_chip(k, slot, s, store):
        for copy in chip_copies(slot, s):
            copy.wait_recv()
        wa, wb, log = pair_weights(l_ref[mine, s], xl[s])
        cl[slot] = jnp.concatenate([log, ld_ref[s]], axis=0)
        for head in range(heads):
            columns = slice(head * HEAD, (head + 1) * HEAD)
            both = (
                o_ref[mine, s, :, columns].astype(jnp.float32) * wa[:, head : head + 1]
                + xo[s, :, columns].astype(jnp.float32) * wb[:, head : head + 1]
            )
            both = jnp.concatenate([both, od_ref[s, :, columns].astype(jnp.float32)], axis=0)
            store[k, :, columns] = both.astype(store.dtype)

    def phase_far(k, carry):
        merge_chip(k, k, far(k), cb)
        for copy in y_copies(k):
            copy.start()
        return carry

    def phase_near(k, carry):
        merge_chip(k, nz + k, near(k), co)
        return carry

    lax.fori_loop(0, nz, phase_far, 0)
    lax.fori_loop(0, nz, phase_near, 0)

    def merge_y(k):
        for copy in y_copies(k):
            copy.wait_recv()
        wa, wb, log = pair_weights(cl[nz + k], yl[k])
        cl[nz + k] = log
        for head in range(heads):
            columns = slice(head * HEAD, (head + 1) * HEAD)
            both = (
                co[k, :, columns] * wa[:, head : head + 1]
                + yb[k, :, columns].astype(jnp.float32) * wb[:, head : head + 1]
            )
            co[k, :, columns] = both
            zb[k, :, columns] = both.astype(jnp.bfloat16)

    def phase_y(k, carry):
        merge_y(k)
        for copy in z_copies(k):
            copy.start()
        return carry

    lax.fori_loop(0, nz - 1, phase_y, 0)
    merge_y(nz - 1)

    def wait_z(k, carry):
        for copy in z_copies(k):
            copy.wait_recv()
        return carry

    lax.fori_loop(0, nz - 1, wait_z, 0)
    logs = [cl[n - 1]] + [rl[k] for k in range(nz - 1)]
    top = functools.reduce(jnp.maximum, logs)
    weights = [jnp.exp(one - top) for one in logs]
    total = functools.reduce(jnp.add, weights)
    weights = [one / total for one in weights]
    for head in range(heads):
        columns = slice(head * HEAD, (head + 1) * HEAD)
        one_column = slice(head, head + 1)
        total = co[nz - 1, :, columns] * weights[0][:, one_column]
        for k in range(nz - 1):
            total = total + rb[k, :, columns].astype(jnp.float32) * weights[k + 1][:, one_column]
        out_ref[me, :, columns] = total.astype(jnp.bfloat16)

    def gather_z(k):
        return send(
            out_ref.at[me], out_ref.at[me], g_send, g_recv, k, {"seq": ahead(k) * 2 + y}
        )

    def forward(k):
        s = lax.rem(z - 1 - k + nz, nz) * 2 + y
        return send(out_ref.at[s], out_ref.at[s], f_send, f_recv, k, {"seq": beside})

    forward_own = send(out_ref.at[me], out_ref.at[me], f_send, f_recv, nz - 1, {"seq": beside})

    def start_gather(k, carry):
        gather_z(k).start()
        return carry

    forward_own.start()
    lax.fori_loop(0, nz - 1, start_gather, 0)

    def pass_on(k, carry):
        gather_z(k).wait_recv()
        forward(k).start()
        return carry

    lax.fori_loop(0, nz - 1, pass_on, 0)

    def finish(k, carry):
        for copy in chip_copies(k, far(k)) + chip_copies(nz + k, near(k)) + y_copies(k):
            copy.wait_send()
        return carry

    def finish_z(k, carry):
        for copy in z_copies(k):
            copy.wait_send()
        gather_z(k).wait_send()
        forward(k).wait()
        return carry

    lax.fori_loop(0, nz, finish, 0)
    lax.fori_loop(0, nz - 1, finish_z, 0)
    forward_own.wait()


def add_kernel(n, p_ref, out_ref, sb, rb, send_sem, recv_sem):
    me = lax.axis_index("tensor")
    barrier = pltpu.get_barrier_semaphore()
    for k in range(1, n):
        pl.semaphore_signal(
            barrier, inc=1, device_id={"tensor": lax.rem(me + k, n)}, device_id_type=MESH
        )
    pl.semaphore_wait(barrier, n - 1)

    def copy(k):
        return pltpu.make_async_remote_copy(
            src_ref=sb.at[k], dst_ref=rb.at[k], send_sem=send_sem.at[k], recv_sem=recv_sem.at[k],
            device_id={"tensor": lax.rem(me + 1 + k, n)}, device_id_type=MESH,
        )

    for k in range(n - 1):
        sb[k] = p_ref[lax.rem(me + 1 + k, n)].astype(jnp.bfloat16)
        copy(k).start()
    for k in range(n - 1):
        copy(k).wait_recv()
    total = p_ref[me]
    for k in range(n - 1):
        total = total + rb[k].astype(jnp.float32)
    out_ref[...] = total.astype(jnp.bfloat16)
    for k in range(n - 1):
        copy(k).wait_send()


def add_tensor(n, partial):
    _, rows, columns = partial.shape
    vmem = pl.BlockSpec(memory_space=pltpu.VMEM)
    return pl.pallas_call(
        functools.partial(add_kernel, n),
        out_shape=jax.ShapeDtypeStruct((rows, columns), jnp.bfloat16),
        in_specs=[vmem],
        out_specs=vmem,
        scratch_shapes=[
            pltpu.VMEM((n - 1, rows, columns), jnp.bfloat16),
            pltpu.VMEM((n - 1, rows, columns), jnp.bfloat16),
            pltpu.SemaphoreType.DMA((n - 1,)),
            pltpu.SemaphoreType.DMA((n - 1,)),
        ],
        compiler_params=pltpu.CompilerParams(
            collective_id=1, has_side_effects=True, vmem_limit_bytes=VMEM_LIMIT
        ),
    )(partial)


def merge(n, o, lse, od, lsed):
    _, _, span_block, width = o.shape
    rows = span_block + od.shape[1]
    vmem = pl.BlockSpec(memory_space=pltpu.VMEM)
    return pl.pallas_call(
        functools.partial(merge_kernel, n, width // HEAD),
        out_shape=jax.ShapeDtypeStruct((n, rows, width), jnp.bfloat16),
        in_specs=[vmem] * 4,
        out_specs=vmem,
        scratch_shapes=[
            pltpu.VMEM((n, span_block, width), jnp.bfloat16),
            pltpu.VMEM((n, span_block, LANES), jnp.float32),
            pltpu.VMEM((n // 2, rows, width), jnp.bfloat16),
            pltpu.VMEM((n, rows, LANES), jnp.float32),
            pltpu.VMEM((n // 2, rows, width), jnp.float32),
            pltpu.VMEM((n // 2, rows, width), jnp.bfloat16),
            pltpu.VMEM((n // 2, rows, LANES), jnp.float32),
            pltpu.VMEM((n // 2, rows, width), jnp.bfloat16),
            pltpu.VMEM((n // 2, rows, width), jnp.bfloat16),
            pltpu.VMEM((n // 2, rows, LANES), jnp.float32),
        ]
        + [pltpu.SemaphoreType.DMA((n,))] * 16,
        compiler_params=pltpu.CompilerParams(
            collective_id=0, has_side_effects=True, vmem_limit_bytes=VMEM_LIMIT
        ),
    )(o, lse, od, lsed)


def body(
    prefill_queries,
    cached_keys,
    cached_values,
    span_keys,
    span_values,
    out_weight,
    decode_queries,
    decode_keys,
    decode_values,
    new_keys,
    new_values,
    request_lengths,
    row_requests,
    block_table,
):
    seq_count = lax.axis_size("seq")
    group_count = lax.axis_size("group")
    seq_index = lax.axis_index("seq")
    owner_index = seq_index * group_count + lax.axis_index("group")
    group_size = HEADS // KV_HEADS
    span_rows, width = prefill_queries.shape
    local_heads = width // HEAD
    local_groups = cached_keys.shape[1] // HEAD
    span_local = span_keys.shape[0]
    span_block = span_rows // (seq_count * group_count)

    both = jnp.concatenate([span_keys, span_values], axis=1)
    gathered = lax.all_gather(both, ("seq", "group"), axis=0, tiled=True)

    first = (owner_index * span_local).astype(jnp.int32).reshape(1)
    o, lse = prefill_local(
        first, prefill_queries, cached_keys, cached_values, span_keys, span_values
    )
    o = o.reshape(group_count, seq_count, span_block, width)
    lse = lse.reshape(group_count, seq_count, span_block, LANES)

    steps, rows_local = decode_queries.shape[:2]
    decode_rows = steps * rows_local
    step_queries = decode_queries.reshape(steps, rows_local, local_groups, group_size, HEAD)
    step_queries = step_queries.transpose(1, 2, 0, 3, 4).reshape(
        rows_local, local_groups, steps * group_size, HEAD
    )
    by_row = lambda x: x.reshape(steps, rows_local, local_groups, HEAD).transpose(1, 2, 0, 3)
    picked = (
        row_requests[:, None] == jnp.arange(request_lengths.shape[0], dtype=jnp.int32)[None, :]
    )
    row_length = jnp.sum(jnp.where(picked, request_lengths[None, :], 0), axis=1)
    od, lsed = decode_local(
        row_length.astype(jnp.int32),
        seq_index.astype(jnp.int32).reshape(1),
        step_queries,
        decode_keys,
        decode_values,
        by_row(new_keys),
        by_row(new_values),
    )
    decode_block = decode_rows // seq_count
    od = od.reshape(rows_local, local_groups, steps, group_size, HEAD)
    od = od.transpose(2, 0, 1, 3, 4).reshape(seq_count, decode_block, width)
    lsed = lsed[..., 0].reshape(rows_local, local_groups, steps, group_size)
    lsed = lsed.transpose(2, 0, 1, 3).reshape(decode_rows, local_heads)
    lsed = jnp.pad(lsed, ((0, 0), (0, LANES - local_heads)))
    lsed = lsed.reshape(seq_count, decode_block, LANES)

    attention = merge(seq_count, o, lse, od, lsed)
    attention = attention.reshape(seq_count * (span_block + decode_block), width)
    partial = jnp.dot(attention, out_weight, preferred_element_type=jnp.float32)
    tensor_count = lax.axis_size("tensor")
    partial = lax.optimization_barrier(partial)
    partial = partial.reshape(partial.shape[0], tensor_count, -1).transpose(1, 0, 2)
    part = add_tensor(tensor_count, partial).reshape(seq_count, span_block + decode_block, -1)
    prefill_out = part[:, :span_block].reshape(seq_count * span_block, -1)
    decode_out = part[:, span_block:].reshape(steps, rows_local, -1)

    block_count = span_rows // BLOCK
    most_blocks = 2 * block_count // (seq_count * group_count)
    targets = block_table[:, 0]
    block_order = jnp.arange(block_count, dtype=jnp.int32)
    earlier = (targets[None, :] == targets[:, None]) & (block_order[None, :] < block_order[:, None])
    block_rank = jnp.sum(earlier.astype(jnp.int32), axis=1)
    slot_ids = jnp.arange(most_blocks, dtype=jnp.int32)
    chosen = (targets[None, :] == owner_index) & (block_rank[None, :] == slot_ids[:, None])
    chosen = chosen.astype(jnp.bfloat16)
    landed = jnp.dot(
        chosen, gathered.reshape(block_count, -1), preferred_element_type=jnp.float32
    ).astype(jnp.bfloat16)
    landed = landed.reshape(1, most_blocks, BLOCK, 2, -1)
    return (prefill_out, decode_out, landed[:, :, :, 0], landed[:, :, :, 1])


def solution(mesh):
    placed = (
        P(None, "tensor"),
        P(("seq", "group"), "tensor"),
        P(("seq", "group"), "tensor"),
        P(("seq", "group"), "tensor"),
        P(("seq", "group"), "tensor"),
        P("tensor", "seq"),
        P(None, "group", "tensor"),
        P("group", "seq", "tensor"),
        P("group", "seq", "tensor"),
        P(None, "group", "tensor"),
        P(None, "group", "tensor"),
        P(),
        P("group"),
        P(),
    )
    return jax.shard_map(
        body,
        mesh=mesh,
        in_specs=placed,
        out_specs=(
            P("group", ("seq", "tensor")),
            P(None, "group", ("seq", "tensor")),
            P(("seq", "group"), None, None, "tensor"),
            P(("seq", "group"), None, None, "tensor"),
        ),
        check_vma=False,
    )
```
